1024 devices in a mesh: fsdp: 32 (over z), bal: 32 (over y, x, core).
Axes of the slice: x: 4, y: 4, z: 32, core: 2. Of those that a mesh axis runs over, the one named last changes fastest.
Arguments:
- query_rows: bfloat16 [1024, 256, 1024], P('fsdp', 'bal'), may hold values from -40 to 40
- key_rows: bfloat16 [1024, 256, 1024], P('fsdp', 'bal'), may hold values from -40 to 40
- value_rows: bfloat16 [1024, 256, 1024], P('fsdp', 'bal'), may hold values from -12 to 12
- cotangent: bfloat16 [1024, 256, 1024], P('fsdp', 'bal'), may hold values from -0.09375 to 0.09375
- out_weight: bfloat16 [1024, 1024], P('fsdp'), may hold values from -0.1875 to 0.1875
- token_counts: int32 [1024, 32], P('fsdp'), may hold values from 0 to 8, as said below
Outputs:
- mixed: bfloat16 [1024, 256, 1024], P('fsdp', 'bal')
- weight_grad: float32 [1024, 1024], P('fsdp')
The draws below stay inside these ranges and needn't reach their ends.
Inputs may be any that keep to these rules, and one draw needn't show every extreme that they name: `token_counts`: every cell has at least one live gene token over all its ranges.
All inputs are finite; a program needn't handle non-finite values.
Results may differ from the reference program's by a relative error of at most 0.015.
Values may be sent and summed in bfloat16 or wider, within the bound.
A program may use at most 32 MiB of HBM per device.

```python
import jax
import jax.numpy as jnp
from jax import lax

D = 1024
HEADS = 8
HEAD_DIM = 128
GENES_DEV = 8
WIDTH_HEADS = 1024
GENES = 256
CELLS = 1024
N_BAL = 32


def draw_query_rows(key, part):
    key = jax.random.fold_in(key, 11)
    width = HEADS * HEAD_DIM
    values = jax.random.truncated_normal(key, -6.0, 6.0, (CELLS, GENES, width), jnp.float32)
    return values.astype(jnp.bfloat16)


def draw_key_rows(key, part):
    key = jax.random.fold_in(key, 13)
    width = HEADS * HEAD_DIM
    values = jax.random.truncated_normal(key, -6.0, 6.0, (CELLS, GENES, width), jnp.float32)
    return values.astype(jnp.bfloat16)


def draw_token_counts(key, part):
    key = jax.random.fold_in(key, 5)
    first_key, second_key = jax.random.split(key)
    third_key = jax.random.fold_in(key, 7)
    cell_index = jnp.arange(CELLS)[:, None]
    ceiling = jax.random.randint(first_key, (CELLS, 1), 1, GENES_DEV + 1)
    ceiling = jnp.where(cell_index % 5 == 0, GENES_DEV, ceiling)
    floor_count = ceiling // 2
    counts = jax.random.randint(second_key, (CELLS, N_BAL), floor_count, ceiling + 1)
    column = jnp.arange(N_BAL)[None, :]
    offset = jax.random.randint(third_key, (CELLS, 1), 1, N_BAL)
    counts = jnp.where(column == cell_index % N_BAL, ceiling, counts)
    counts = jnp.where(column == (cell_index + offset) % N_BAL, 0, counts)
    return counts.astype(jnp.int32)


def spiked(array, own_key, source, target, blocks, factor):
    owner, partner = [(jnp.arange(array.shape[dim]) // (array.shape[dim] // blocks)).reshape([-1 if axis == dim else 1 for axis in range(array.ndim)]) for dim in (source, target)]
    chosen = jax.random.permutation(own_key, blocks)[partner]
    strong = (owner == chosen) | (owner == (partner + blocks // 2) % blocks)
    return jnp.where(strong, factor * array, array)


def shard_levels(own_key, shape, cuts, low, largest):
    level = 1.0
    for axis_at, shards_of in cuts:
        heights = jax.random.uniform(jax.random.fold_in(jax.random.fold_in(own_key, 6), axis_at), (shards_of,), jnp.float32, low / len(cuts), largest / len(cuts))
        level = level * jnp.repeat(jnp.exp(heights), shape[axis_at] // shards_of).reshape((-1,) + (1,) * (len(shape) - 1 - axis_at))
    return level


def normal_values(key, shape, deviation, most, pieces=(), held_as=jnp.bfloat16):
    entries = jax.random.normal(key, shape, jnp.float32) * deviation
    if len(pieces) > 0:
        entries = shard_levels(key, shape, pieces, -0.22, 0.18) * entries
    return jnp.clip(entries, min=-most, max=most).astype(held_as)


def bell_draw_with(stream_key, dims, spread, reach, pieces, heavy, kind=jnp.bfloat16):
    result = spread * jax.random.normal(stream_key, dims, jnp.float32)
    if pieces:
        result = result * shard_levels(stream_key, dims, pieces, -0.22, 0.18)
    return jnp.clip(spiked(result, jax.random.fold_in(stream_key, 3), *heavy), -reach, reach).astype(kind)


def setup_inputs(seed: int = 0) -> dict:
    key_of = jax.random.split(jax.random.key(seed), 7)
    query_rows = draw_query_rows(jax.random.fold_in(key_of[6], 71), 0)
    key_rows = draw_key_rows(jax.random.fold_in(key_of[6], 71), 0)
    value_rows = normal_values(key_of[2], (CELLS, GENES, WIDTH_HEADS), 2.0, 12.0, ((0, 32), (1, 32)))
    cotangent = bell_draw_with(key_of[3], (CELLS, GENES, D), (4.0 * (CELLS * GENES) ** -0.5), 0.09375, ((0, 32), (1, 32)), (0, 2, 32, 2.75))
    out_weight = normal_values(key_of[4], (D, WIDTH_HEADS), WIDTH_HEADS ** -0.5, 0.1875, ((0, 32),))
    token_counts = draw_token_counts(jax.random.fold_in(key_of[6], 71), 0)
    return dict(query_rows=query_rows, key_rows=key_rows, value_rows=value_rows, cotangent=cotangent, out_weight=out_weight, token_counts=token_counts)


def attend_block(query_block, key_block, value_block, live_block):
    cells, slots, width = query_block.shape
    shape_heads = (cells, slots, HEADS, HEAD_DIM)
    query_float = query_block.astype(jnp.float32).reshape(shape_heads)
    key_float = key_block.astype(jnp.float32).reshape(shape_heads)
    value_float = value_block.astype(jnp.float32).reshape(shape_heads)
    scores = jnp.einsum('cqhd,ckhd->chqk', query_float, key_float) * (HEAD_DIM ** -0.5)
    scores = jnp.where(live_block[:, None, None, :], scores, -1e30)
    peak = jnp.max(scores, axis=-1, keepdims=True)
    expo = jnp.exp(scores - peak)
    probs = (expo / jnp.sum(expo, axis=-1, keepdims=True)).astype(jnp.bfloat16)
    attended = jnp.einsum('chqk,ckhd->cqhd', probs.astype(jnp.float32), value_float)
    attended = jnp.where(live_block[:, :, None, None], attended, 0.0)
    return attended.reshape(cells, slots, width).astype(jnp.bfloat16)


def reference(query_rows, key_rows, value_rows, cotangent, out_weight, token_counts):
    slot_range = (jnp.arange(GENES) % GENES_DEV).astype(jnp.int32)
    live = slot_range[None, :] < jnp.repeat(token_counts, GENES_DEV, axis=1)
    blocks = CELLS // N_BAL
    width = HEADS * HEAD_DIM
    shaped = (blocks, N_BAL, GENES, width)

    def one_block(parts):
        return attend_block(parts[0], parts[1], parts[2], parts[3])

    attended = lax.map(one_block, (query_rows.reshape(shaped), key_rows.reshape(shaped),
                                   value_rows.reshape(shaped), live.reshape(blocks, N_BAL, GENES)))
    attended_flat = attended.reshape(CELLS * GENES, width)
    mixed = jnp.dot(attended_flat, out_weight.T, preferred_element_type=jnp.float32)
    mixed = mixed.astype(jnp.bfloat16).reshape(CELLS, GENES, D)
    weight_grad = jnp.dot(cotangent.reshape(CELLS * GENES, D).T, attended_flat,
                          preferred_element_type=jnp.float32)
    return mixed, weight_grad
```

```python
import functools

import jax
import jax.numpy as jnp
from jax import lax
from jax.experimental import pallas as pl
from jax.experimental.pallas import tpu as pltpu
from jax.sharding import PartitionSpec as P

HEAD_DIM = 128
GROUPS = 4
MESH = pl.DeviceIdType.MESH
BF16 = jnp.bfloat16
F32 = jnp.float32


def remote(src, dst, send_sem, recv_sem, target):
    return pltpu.make_async_remote_copy(
        src_ref=src,
        dst_ref=dst,
        send_sem=send_sem,
        recv_sem=recv_sem,
        device_id=target,
        device_id_type=MESH,
    )


def await_bytes(ref, sem):
    pltpu.make_async_copy(ref, ref, sem).wait()


def flat_rows(block):
    cells, genes, cols = block.shape
    return block.astype(F32).reshape(cells * genes, cols).astype(BF16)


def kernel(
    nz, nb, q, k, v, cot, w, counts, mixed_out, grad_out,
    qkv, att_s, att_h, cot_v, cot_p, wbuf, counts_v, mixed_v, att_2d,
    mine, pair_s, pair_r, rs_s, rs_r, z_32, z_s, z_r, row_s, row_r, grad_v,
    s_qkv, r_qkv, s_att, r_att, s_ring, r_right, r_left, s_sib, r_sib,
    s_pair, r_pair, s_rs, r_rs, s_z, r_z, s_row, r_row, local_sem, out_sem,
):
    my_z, me = lax.axis_index("fsdp"), lax.axis_index("bal")
    core, chip = lax.rem(me, 2), me // 2
    sibling = {"bal": chip * 2 + (1 - core)}
    chips = nb // 2
    width = qkv.shape[-1]
    group_cols = width // GROUPS
    heads_per = group_cols // HEAD_DIM
    half = w.shape[0] // 2
    rows = nb * 8
    features = nz * nb

    def cols_of(g):
        return pl.ds(pl.multiple_of(g * group_cols, group_cols), group_cols)

    barrier = pltpu.get_barrier_semaphore()

    @pl.loop(1, nb)
    def _(i):
        pl.semaphore_signal(barrier, 1, device_id={"bal": lax.rem(me + i, nb)}, device_id_type=MESH)

    @pl.loop(1, nz)
    def _(i):
        pl.semaphore_signal(barrier, 1, device_id={"fsdp": lax.rem(my_z + i, nz)}, device_id_type=MESH)

    load_cot = pltpu.make_async_copy(cot, cot_v, local_sem.at[0])
    load_counts = pltpu.make_async_copy(counts, counts_v, local_sem.at[1])
    load_w0 = pltpu.make_async_copy(w.at[pl.ds(0, half)], wbuf.at[my_z, 0], local_sem.at[2])
    load_w1 = pltpu.make_async_copy(w.at[pl.ds(half, half)], wbuf.at[my_z, 1], local_sem.at[3])
    for load in (load_cot, load_counts, load_w0, load_w1):
        load.start()

    pl.semaphore_wait(barrier, nb + nz - 2)
    load_w0.wait()
    load_w1.wait()

    right, left = {"fsdp": lax.rem(my_z + 1, nz)}, {"fsdp": lax.rem(my_z + nz - 1, nz)}
    right_hops, left_hops = nz // 2, nz // 2 - 1

    def ring_right(step):
        block = wbuf.at[lax.rem(my_z + nz - step, nz), core]
        remote(block, block, s_ring, r_right.at[step], right).start()

    def ring_left(step):
        block = wbuf.at[lax.rem(my_z + step, nz), core]
        remote(block, block, s_ring, r_left.at[step], left).start()

    def ring_step(step):
        block = wbuf.at[lax.rem(my_z + nz - step, nz), core]
        await_bytes(block, r_right.at[step - 1])

        @pl.when(step < right_hops)
        def _():
            ring_right(step)

        remote(block, block, s_sib, r_sib, sibling).start()

        @pl.when(step <= left_hops)
        def _():
            other = wbuf.at[lax.rem(my_z + step, nz), core]
            await_bytes(other, r_left.at[step - 1])

            @pl.when(step < left_hops)
            def _():
                ring_left(step)

            remote(other, other, s_sib, r_sib, sibling).start()

    ring_right(0)
    ring_left(0)

    for g in range(GROUPS):
        cols = pl.ds(g * group_cols, group_cols)
        for a, ref in enumerate((q, k, v)):
            pltpu.make_async_copy(ref.at[me, :, cols], qkv.at[a, me, :, cols], r_qkv.at[g]).start()

        @pl.loop(1, nb)
        def _(i):
            peer = lax.rem(me + i, nb)
            for a, ref in enumerate((q, k, v)):
                remote(
                    ref.at[peer, :, cols], qkv.at[a, me, :, cols], s_qkv, r_qkv.at[g], {"bal": peer}
                ).start()

    load_cot.wait()
    load_counts.wait()
    cot_2d = flat_rows(cot_v[...])
    step_rows = min(256, features)

    @pl.loop(0, features // step_rows)
    def _(n):
        shape = (step_rows, features)
        m = lax.broadcasted_iota(jnp.int32, shape, 0) + n * step_rows
        f = lax.broadcasted_iota(jnp.int32, shape, 1)
        source = (m % nz) * nb + ((m // nz) % chips) * 2 + m // (nz * chips)
        chosen = jnp.where(f == source, 1.0, 0.0).astype(BF16)
        out = lax.dot_general(chosen, cot_2d, (((1,), (1,)), ((), ())), preferred_element_type=F32)
        cot_p[pl.ds(pl.multiple_of(n * step_rows, step_rows), step_rows), :] = out.astype(BF16)

    my_counts = counts_v[pl.ds(me, 1), :].astype(F32)
    spread = lax.broadcasted_iota(jnp.int32, (rows, nb), 0) // 8 == lax.broadcasted_iota(
        jnp.int32, (rows, nb), 1
    )
    picked = jnp.where(spread, jnp.broadcast_to(my_counts, (rows, nb)), 0.0)
    row_count = jnp.sum(picked, axis=1, keepdims=True)
    slot = (lax.broadcasted_iota(jnp.int32, (rows, 1), 0) % 8).astype(F32)
    row_live = slot < row_count
    gather = (
        lax.broadcasted_iota(jnp.int32, (nb, rows), 1) // 8 == lax.broadcasted_iota(jnp.int32, (nb, rows), 0)
    )
    col_count = lax.dot_general(
        jnp.broadcast_to(my_counts, (8, nb)).astype(BF16),
        jnp.where(gather, 1.0, 0.0).astype(BF16),
        (((1,), (0,)), ((), ())),
        preferred_element_type=F32,
    )[0:1, :]
    col_slot = (lax.broadcasted_iota(jnp.int32, (1, rows), 1) % 8).astype(F32)
    col_live = col_slot < col_count
    scale = HEAD_DIM ** (-0.5)

    ring_per = -(-right_hops // GROUPS)

    def ring_some(g):
        for j in range(ring_per):
            step = g * ring_per + j + 1

            @pl.when(step <= right_hops)
            def _():
                ring_step(step)

    @pl.loop(0, GROUPS)
    def _(g):
        ring_some(g)
        cols = cols_of(g)
        await_bytes(qkv.at[:, :, :, cols], r_qkv.at[g])
        for h in range(heads_per):
            head = pl.ds(pl.multiple_of(g * group_cols + h * HEAD_DIM, HEAD_DIM), HEAD_DIM)
            qh = flat_rows(qkv[0, :, :, head])
            kh = flat_rows(qkv[1, :, :, head])
            vh = flat_rows(qkv[2, :, :, head])
            scores = lax.dot_general(qh, kh, (((1,), (1,)), ((), ())), preferred_element_type=F32)
            scores = jnp.where(col_live, scores * scale, -1e30)
            peak = jnp.max(scores, axis=1, keepdims=True)
            expo = jnp.exp(scores - peak)
            total = jnp.sum(expo, axis=1, keepdims=True)
            probs = (expo * (1.0 / total)).astype(BF16)
            out = lax.dot_general(probs, vh, (((1,), (0,)), ((), ())), preferred_element_type=F32)
            out = jnp.where(row_live, out, 0.0)
            att_s[:, :, head] = out.reshape(nb, 8, HEAD_DIM).astype(BF16)
        pltpu.make_async_copy(att_s.at[me, :, cols], att_h.at[me, :, cols], r_att.at[g]).start()

        @pl.loop(1, nb)
        def _(i):
            peer = lax.rem(me + i, nb)
            remote(
                att_s.at[peer, :, cols], att_h.at[me, :, cols], s_att, r_att.at[g], {"bal": peer}
            ).start()

    half_rows = features // 2

    @pl.loop(0, GROUPS)
    def _(g):
        cols = cols_of(g)
        await_bytes(att_h.at[:, :, cols], r_att.at[g])
        a2 = flat_rows(att_h[:, :, cols])
        att_2d[:, cols] = a2
        their_rows = pl.ds(pl.multiple_of((1 - core) * half_rows, half_rows), half_rows)
        pair_s[g] = jnp.dot(cot_p[their_rows, :], a2, preferred_element_type=F32).astype(BF16)
        remote(pair_s.at[g], pair_r.at[g], s_pair, r_pair.at[g], sibling).start()
        my_rows = pl.ds(pl.multiple_of(core * half_rows, half_rows), half_rows)
        mine[g] = jnp.dot(cot_p[my_rows, :], a2, preferred_element_type=F32)

    @pl.loop(0, GROUPS)
    def _(g):
        await_bytes(pair_r.at[g], r_pair.at[g])
        both = mine[g] + pair_r[g].astype(F32)
        rs_s[g] = both.reshape(chips, nz, group_cols).astype(BF16)
        pltpu.make_async_copy(rs_s.at[g, chip], rs_r.at[g, chip], r_rs.at[g]).start()

        @pl.loop(1, chips)
        def _(i):
            peer = lax.rem(chip + i, chips)
            remote(
                rs_s.at[g, peer], rs_r.at[g, chip], s_rs, r_rs.at[g], {"bal": peer * 2 + core}
            ).start()

    await_bytes(wbuf.at[pl.ds(0, nz - 1), 0], r_sib)
    blocks = 8 if nz % 8 == 0 else nz
    out_cols = blocks * 2 * half

    @pl.loop(0, nz // blocks)
    def _(n):
        wn = wbuf[pl.ds(n * blocks, blocks)].reshape(out_cols, width)
        out = lax.dot_general(att_2d[...], wn, (((1,), (1,)), ((), ())), preferred_element_type=F32)
        out_at = pl.ds(pl.multiple_of(n * out_cols, out_cols), out_cols)
        mixed_v[:, :, out_at] = out.reshape(nb, 8, out_cols).astype(BF16)

    store_mixed = pltpu.make_async_copy(mixed_v, mixed_out, out_sem.at[0])
    store_mixed.start()

    for g in range(GROUPS):
        await_bytes(rs_r.at[g], r_rs.at[g])
        plane = jnp.sum(rs_r[g].astype(F32), axis=0)
        for t in range(group_cols // 128):
            z_32[pl.ds(g * (group_cols // 128) + t, nz, stride=8), :] = plane[:, t * 128 : (t + 1) * 128]
    z_s[...] = z_32[...].reshape(nz, 8, 128).astype(BF16)
    pltpu.make_async_copy(z_s.at[my_z], z_r.at[my_z], r_z).start()

    @pl.loop(1, nz)
    def _(i):
        peer = lax.rem(my_z + i, nz)
        remote(z_s.at[peer], z_r.at[my_z], s_z, r_z, {"fsdp": peer}).start()

    await_bytes(z_r, r_z)
    row_s[...] = jnp.sum(z_r[...].astype(F32), axis=0)
    pltpu.make_async_copy(row_s, row_r.at[me], r_row).start()

    @pl.loop(1, nb)
    def _(i):
        peer = lax.rem(me + i, nb)
        remote(row_s, row_r.at[me], s_row, r_row, {"bal": peer}).start()

    await_bytes(row_r, r_row)
    for t in range(8):
        grad_v[:, t * 128 : (t + 1) * 128] = row_r[:, t, :]
    store_grad = pltpu.make_async_copy(grad_v, grad_out, out_sem.at[1])
    store_grad.start()

    await_bytes(qkv.at[:, pl.ds(0, nb - 1)], s_qkv)
    await_bytes(att_s.at[pl.ds(0, nb - 1)], s_att)
    await_bytes(wbuf.at[pl.ds(0, nz - 1), 0], s_ring)
    await_bytes(wbuf.at[pl.ds(0, nz - 1), 0], s_sib)
    await_bytes(pair_s, s_pair)
    await_bytes(rs_s.at[:, pl.ds(0, chips - 1)], s_rs)
    await_bytes(z_s.at[pl.ds(0, nz - 1)], s_z)
    await_bytes(row_r.at[pl.ds(0, nb - 1)], s_row)
    store_mixed.wait()
    store_grad.wait()


def local(nz, nb, query_rows, key_rows, value_rows, cotangent, out_weight, token_counts):
    cells, genes, width = query_rows.shape
    shard = out_weight.shape[0]
    features = nz * shard
    rows = cells * genes
    group_cols = width // GROUPS
    chips = nb // 2
    vmem = pltpu.VMEM
    dma = pltpu.SemaphoreType.DMA
    scratch = [
        vmem((3, nb, genes, width), BF16),
        vmem((nb, genes, width), BF16),
        vmem((nb, genes, width), BF16),
        vmem((nb, genes, features), BF16),
        vmem((features, rows), BF16),
        vmem((nz, 2, shard // 2, width), BF16),
        vmem(token_counts.shape, jnp.int32),
        vmem((nb, genes, features), BF16),
        vmem((rows, width), BF16),
        vmem((GROUPS, features // 2, group_cols), F32),
        vmem((GROUPS, features // 2, group_cols), BF16),
        vmem((GROUPS, features // 2, group_cols), BF16),
        vmem((GROUPS, chips, nz, group_cols), BF16),
        vmem((GROUPS, chips, nz, group_cols), BF16),
        vmem((nz * 8, 128), F32),
        vmem((nz, 8, 128), BF16),
        vmem((nz, 8, 128), BF16),
        vmem((8, 128), F32),
        vmem((nb, 8, 128), F32),
        vmem((shard, width), F32),
        dma, dma((GROUPS,)),
        dma, dma((GROUPS,)),
        dma, dma((nz // 2,)), dma((nz // 2,)),
        dma, dma,
        dma, dma((GROUPS,)),
        dma, dma((GROUPS,)),
        dma, dma,
        dma, dma,
        dma((4,)),
        dma((2,)),
    ]
    any_spec = pl.BlockSpec(memory_space=pl.ANY)
    return pl.pallas_call(
        functools.partial(kernel, nz, nb),
        out_shape=(
            jax.ShapeDtypeStruct((cells, genes, features), BF16),
            jax.ShapeDtypeStruct((shard, width), F32),
        ),
        in_specs=[any_spec] * 6,
        out_specs=(any_spec, any_spec),
        scratch_shapes=scratch,
        compiler_params=pltpu.CompilerParams(
            collective_id=0, has_side_effects=True, vmem_limit_bytes=48 * 1024 * 1024
        ),
        name="attend_project",
    )(query_rows, key_rows, value_rows, cotangent, out_weight, token_counts)


def solution(mesh):
    nz, nb = mesh.shape["fsdp"], mesh.shape["bal"]
    placed = (
        P("fsdp", "bal", None),
        P("fsdp", "bal", None),
        P("fsdp", "bal", None),
        P("fsdp", "bal", None),
        P("fsdp", None),
        P("fsdp", None),
    )
    return jax.shard_map(
        functools.partial(local, nz, nb),
        mesh=mesh,
        in_specs=placed,
        out_specs=(P("fsdp", "bal", None), P("fsdp", None)),
        check_vma=False,
    )
```

```python
import functools

import jax
import jax.numpy as jnp
from jax import lax
from jax.experimental import pallas as pl
from jax.experimental.pallas import tpu as pltpu
from jax.sharding import PartitionSpec as P

HEAD_DIM = 128
GROUPS = 4
MESH = pl.DeviceIdType.MESH
BF16 = jnp.bfloat16
F32 = jnp.float32


def remote(src, dst, send_sem, recv_sem, target):
    return pltpu.make_async_remote_copy(
        src_ref=src,
        dst_ref=dst,
        send_sem=send_sem,
        recv_sem=recv_sem,
        device_id=target,
        device_id_type=MESH,
    )


def await_bytes(ref, sem):
    pltpu.make_async_copy(ref, ref, sem).wait()


def flat_rows(block):
    cells, genes, cols = block.shape
    return block.astype(F32).reshape(cells * genes, cols).astype(BF16)


def far_first(i, n):
    return n // 2 + ((i + 1) // 2) * (1 - 2 * (i % 2))


def kernel(
    nz, nb, q, k, v, cot, w, counts, mixed_out, grad_out,
    stage, qkv, att_s, att_h, cot_v, cot_p, w_v, w_st, wz, wfull, counts_v, mixed_v, att_2d,
    mine, pair_s, pair_r, rs_s, rs_r, z_32, z_s, z_r, row_s, row_r, grad_v,
    s_qkv, r_qkv, s_att, r_att, s_wz, r_wz, s_wa, r_wa, s_sib, r_sib,
    s_pair, r_pair, s_rs, r_rs, s_z, r_z, s_row, r_row, local_sem, out_sem,
):
    my_z, me = lax.axis_index("fsdp"), lax.axis_index("bal")
    core, chip = lax.rem(me, 2), me // 2
    sibling = {"bal": chip * 2 + (1 - core)}
    chips = nb // 2
    width = qkv.shape[-1]
    group_cols = width // GROUPS
    heads_per = group_cols // HEAD_DIM
    half_width = width // 2
    rows = nb * 8
    features = nz * nb

    def cols_of(g):
        return pl.ds(pl.multiple_of(g * group_cols, group_cols), group_cols)

    barrier = pltpu.get_barrier_semaphore()

    @pl.loop(1, nb)
    def _(i):
        pl.semaphore_signal(barrier, 1, device_id={"bal": lax.rem(me + i, nb)}, device_id_type=MESH)

    @pl.loop(1, nz)
    def _(i):
        pl.semaphore_signal(barrier, 1, device_id={"fsdp": lax.rem(my_z + i, nz)}, device_id_type=MESH)

    loads = [
        pltpu.make_async_copy(ref, stage.at[:, a], local_sem.at[a]) for a, ref in enumerate((q, k, v))
    ]
    load_w = pltpu.make_async_copy(w, w_v, local_sem.at[3])
    load_cot = pltpu.make_async_copy(cot, cot_v, local_sem.at[4])
    load_counts = pltpu.make_async_copy(counts, counts_v, local_sem.at[5])
    for load in (*loads, load_w, load_cot, load_counts):
        load.start()

    load_w.wait()
    shard = w_v[...].astype(F32)
    for a in range(w_v.shape[0] // 8):
        for t in range(width // 128):
            w_st[a, t] = shard[a * 8 : a * 8 + 8, t * 128 : t * 128 + 128].astype(BF16)
    tile_row, tile_col = chip // 4, chip % 4 + 4 * core
    for load in loads:
        load.wait()
    pl.semaphore_wait(barrier, nb + nz - 2)

    def send_qkv(g):
        cols = cols_of(g)
        pltpu.make_async_copy(stage.at[me, :, :, cols], qkv.at[me, :, :, cols], r_qkv.at[g]).start()

        @pl.loop(1, nb)
        def _(i):
            peer = lax.rem(me + i, nb)
            remote(
                stage.at[peer, :, :, cols], qkv.at[me, :, :, cols], s_qkv, r_qkv.at[g], {"bal": peer}
            ).start()

    send_qkv(0)
    pltpu.make_async_copy(w_st.at[tile_row, tile_col], wz.at[my_z], r_wz).start()

    @pl.loop(0, nz - 1)
    def _(i):
        peer = lax.rem(my_z + far_first(i, nz), nz)
        remote(w_st.at[tile_row, tile_col], wz.at[my_z], s_wz, r_wz, {"fsdp": peer}).start()

    send_qkv(1)

    load_cot.wait()
    load_counts.wait()
    cot_2d = flat_rows(cot_v[...])
    step_rows = min(256, features)

    @pl.loop(0, features // step_rows)
    def _(n):
        shape = (step_rows, features)
        m = lax.broadcasted_iota(jnp.int32, shape, 0) + n * step_rows
        f = lax.broadcasted_iota(jnp.int32, shape, 1)
        source = (m % nz) * nb + ((m // nz) % chips) * 2 + m // (nz * chips)
        chosen = jnp.where(f == source, 1.0, 0.0).astype(BF16)
        out = lax.dot_general(chosen, cot_2d, (((1,), (1,)), ((), ())), preferred_element_type=F32)
        cot_p[pl.ds(pl.multiple_of(n * step_rows, step_rows), step_rows), :] = out.astype(BF16)

    my_counts = counts_v[pl.ds(me, 1), :].astype(F32)
    spread = lax.broadcasted_iota(jnp.int32, (rows, nb), 0) // 8 == lax.broadcasted_iota(
        jnp.int32, (rows, nb), 1
    )
    picked = jnp.where(spread, jnp.broadcast_to(my_counts, (rows, nb)), 0.0)
    row_count = jnp.sum(picked, axis=1, keepdims=True)
    slot = (lax.broadcasted_iota(jnp.int32, (rows, 1), 0) % 8).astype(F32)
    row_live = slot < row_count
    gather = (
        lax.broadcasted_iota(jnp.int32, (nb, rows), 1) // 8 == lax.broadcasted_iota(jnp.int32, (nb, rows), 0)
    )
    col_count = lax.dot_general(
        jnp.broadcast_to(my_counts, (8, nb)).astype(BF16),
        jnp.where(gather, 1.0, 0.0).astype(BF16),
        (((1,), (0,)), ((), ())),
        preferred_element_type=F32,
    )[0:1, :]
    col_slot = (lax.broadcasted_iota(jnp.int32, (1, rows), 1) % 8).astype(F32)
    col_live = col_slot < col_count
    scale = HEAD_DIM ** (-0.5)
    half_rows = features // 2

    def attend(g):
        cols = cols_of(g)
        await_bytes(qkv.at[:, :, :, cols], r_qkv.at[g])
        for h in range(heads_per):
            head = pl.ds(pl.multiple_of(g * group_cols + h * HEAD_DIM, HEAD_DIM), HEAD_DIM)
            qh = flat_rows(qkv[:, 0, :, head])
            kh = flat_rows(qkv[:, 1, :, head])
            vh = flat_rows(qkv[:, 2, :, head])
            scores = lax.dot_general(qh, kh, (((1,), (1,)), ((), ())), preferred_element_type=F32)
            scores = jnp.where(col_live, scores * scale, -1e30)
            peak = jnp.max(scores, axis=1, keepdims=True)
            expo = jnp.exp(scores - peak)
            total = jnp.sum(expo, axis=1, keepdims=True)
            probs = (expo * (1.0 / total)).astype(BF16)
            out = lax.dot_general(probs, vh, (((1,), (0,)), ((), ())), preferred_element_type=F32)
            out = jnp.where(row_live, out, 0.0)
            att_s[:, :, head] = out.reshape(nb, 8, HEAD_DIM).astype(BF16)
        pltpu.make_async_copy(att_s.at[me, :, cols], att_h.at[me, :, cols], r_att.at[g]).start()

        @pl.loop(1, nb)
        def _(i):
            peer = lax.rem(me + i, nb)
            remote(
                att_s.at[peer, :, cols], att_h.at[me, :, cols], s_att, r_att.at[g], {"bal": peer}
            ).start()

    def share(g):
        cols = cols_of(g)
        await_bytes(att_h.at[:, :, cols], r_att.at[g])
        a2 = flat_rows(att_h[:, :, cols])
        att_2d[:, cols] = a2
        their_rows = pl.ds(pl.multiple_of((1 - core) * half_rows, half_rows), half_rows)
        pair_s[g] = jnp.dot(cot_p[their_rows, :], a2, preferred_element_type=F32).astype(BF16)
        remote(pair_s.at[g], pair_r.at[g], s_pair, r_pair.at[g], sibling).start()
        my_rows = pl.ds(pl.multiple_of(core * half_rows, half_rows), half_rows)
        mine[g] = jnp.dot(cot_p[my_rows, :], a2, preferred_element_type=F32)

    def scatter(g):
        await_bytes(pair_r.at[g], r_pair.at[g])
        both = mine[g] + pair_r[g].astype(F32)
        rs_s[g] = both.reshape(chips, nz, group_cols).astype(BF16)
        pltpu.make_async_copy(rs_s.at[g, chip], rs_r.at[g, chip], r_rs.at[g]).start()

        @pl.loop(1, chips)
        def _(i):
            peer = lax.rem(chip + i, chips)
            remote(
                rs_s.at[g, peer], rs_r.at[g, chip], s_rs, r_rs.at[g], {"bal": peer * 2 + core}
            ).start()

    @pl.loop(0, GROUPS + 2)
    def _(t):
        @pl.when(t < GROUPS)
        def _():
            attend(t)

        @pl.when(t + 2 < GROUPS)
        def _():
            send_qkv(t + 2)

        @pl.when(t >= 2)
        def _():
            scatter(t - 2)

        @pl.when(jnp.logical_and(t >= 1, t < GROUPS + 1))
        def _():
            share(t - 1)

    await_bytes(wz, r_wz)
    tile = wfull.at[:, tile_row, :, pl.ds(pl.multiple_of(tile_col * 128, 128), 128)]
    pltpu.make_async_copy(wz, tile, r_wa).start()

    @pl.loop(1, chips)
    def _(i):
        peer = lax.rem(chip + i, chips)
        remote(wz, tile, s_wa, r_wa, {"bal": peer * 2 + core}).start()

    for g in range(GROUPS):
        await_bytes(rs_r.at[g], r_rs.at[g])
        plane = jnp.sum(rs_r[g].astype(F32), axis=0)
        for t in range(group_cols // 128):
            z_32[pl.ds(g * (group_cols // 128) + t, nz, stride=8), :] = plane[:, t * 128 : (t + 1) * 128]
    z_s[...] = z_32[...].reshape(nz, 8, 128).astype(BF16)
    pltpu.make_async_copy(z_s.at[my_z], z_r.at[my_z], r_z).start()

    @pl.loop(0, nz - 1)
    def _(i):
        peer = lax.rem(my_z + far_first(i, nz), nz)
        remote(z_s.at[peer], z_r.at[my_z], s_z, r_z, {"fsdp": peer}).start()

    my_half = wfull.at[:, :, :, pl.ds(pl.multiple_of(core * half_width, half_width), half_width)]
    await_bytes(my_half, r_wa)
    remote(my_half, my_half, s_sib, r_sib, sibling).start()

    await_bytes(z_r, r_z)
    row_s[...] = jnp.sum(z_r[...].astype(F32), axis=0)
    pltpu.make_async_copy(row_s, row_r.at[me], r_row).start()

    @pl.loop(1, nb)
    def _(i):
        peer = lax.rem(me + i, nb)
        remote(row_s, row_r.at[me], s_row, r_row, {"bal": peer}).start()

    await_bytes(my_half, r_sib)
    blocks = 8 if nz % 8 == 0 else nz
    out_cols = blocks * nb

    @pl.loop(0, nz // blocks)
    def _(n):
        wn = wfull[pl.ds(n * blocks, blocks)].astype(F32).reshape(out_cols, width).astype(BF16)
        out = lax.dot_general(att_2d[...], wn, (((1,), (1,)), ((), ())), preferred_element_type=F32)
        out_at = pl.ds(pl.multiple_of(n * out_cols, out_cols), out_cols)
        mixed_v[:, :, out_at] = out.reshape(nb, 8, out_cols).astype(BF16)

    store_mixed = pltpu.make_async_copy(mixed_v, mixed_out, out_sem.at[0])
    store_mixed.start()

    await_bytes(row_r, r_row)
    for t in range(8):
        grad_v[:, t * 128 : (t + 1) * 128] = row_r[:, t, :]
    store_grad = pltpu.make_async_copy(grad_v, grad_out, out_sem.at[1])
    store_grad.start()

    await_bytes(qkv.at[pl.ds(0, nb - 1)], s_qkv)
    await_bytes(att_s.at[pl.ds(0, nb - 1)], s_att)
    await_bytes(wz.at[pl.ds(0, nz - 1)], s_wz)
    await_bytes(rs_r.at[:, pl.ds(0, chips - 1)], s_wa)
    await_bytes(my_half, s_sib)
    await_bytes(pair_s, s_pair)
    await_bytes(rs_s.at[:, pl.ds(0, chips - 1)], s_rs)
    await_bytes(z_s.at[pl.ds(0, nz - 1)], s_z)
    await_bytes(row_r.at[pl.ds(0, nb - 1)], s_row)
    store_mixed.wait()
    store_grad.wait()


def local(nz, nb, query_rows, key_rows, value_rows, cotangent, out_weight, token_counts):
    cells, genes, width = query_rows.shape
    shard = out_weight.shape[0]
    features = nz * shard
    rows = cells * genes
    group_cols = width // GROUPS
    chips = nb // 2
    vmem = pltpu.VMEM
    dma = pltpu.SemaphoreType.DMA
    scratch = [
        vmem((nb, 3, genes, width), BF16),
        vmem((nb, 3, genes, width), BF16),
        vmem((nb, genes, width), BF16),
        vmem((nb, genes, width), BF16),
        vmem((nb, genes, features), BF16),
        vmem((features, rows), BF16),
        vmem((shard, width), BF16),
        vmem((shard // 8, width // 128, 8, 128), BF16),
        vmem((nz, 8, 128), BF16),
        vmem((nz, shard // 8, 8, width), BF16),
        vmem(token_counts.shape, jnp.int32),
        vmem((nb, genes, features), BF16),
        vmem((rows, width), BF16),
        vmem((GROUPS, features // 2, group_cols), F32),
        vmem((GROUPS, features // 2, group_cols), BF16),
        vmem((GROUPS, features // 2, group_cols), BF16),
        vmem((GROUPS, chips, nz, group_cols), BF16),
        vmem((GROUPS, chips, nz, group_cols), BF16),
        vmem((nz * 8, 128), F32),
        vmem((nz, 8, 128), BF16),
        vmem((nz, 8, 128), BF16),
        vmem((8, 128), F32),
        vmem((nb, 8, 128), F32),
        vmem((shard, width), F32),
        dma, dma((GROUPS,)),
        dma, dma((GROUPS,)),
        dma, dma,
        dma, dma,
        dma, dma,
        dma, dma((GROUPS,)),
        dma, dma((GROUPS,)),
        dma, dma,
        dma, dma,
        dma((6,)),
        dma((2,)),
    ]
    any_spec = pl.BlockSpec(memory_space=pl.ANY)
    return pl.pallas_call(
        functools.partial(kernel, nz, nb),
        out_shape=(
            jax.ShapeDtypeStruct((cells, genes, features), BF16),
            jax.ShapeDtypeStruct((shard, width), F32),
        ),
        in_specs=[any_spec] * 6,
        out_specs=(any_spec, any_spec),
        scratch_shapes=scratch,
        compiler_params=pltpu.CompilerParams(
            collective_id=0, has_side_effects=True, vmem_limit_bytes=48 * 1024 * 1024
        ),
        name="attend_project",
    )(*[pltpu.with_memory_space_constraint(a, pltpu.HBM) for a in (query_rows, key_rows, value_rows, cotangent, out_weight, token_counts)])


def solution(mesh):
    nz, nb = mesh.shape["fsdp"], mesh.shape["bal"]
    placed = (
        P("fsdp", "bal", None),
        P("fsdp", "bal", None),
        P("fsdp", "bal", None),
        P("fsdp", "bal", None),
        P("fsdp", None),
        P("fsdp", None),
    )
    return jax.shard_map(
        functools.partial(local, nz, nb),
        mesh=mesh,
        in_specs=placed,
        out_specs=(P("fsdp", "bal", None), P("fsdp", None)),
        check_vma=False,
    )
```

```python
import functools

import jax
import jax.numpy as jnp
from jax import lax
from jax.experimental import pallas as pl
from jax.experimental.pallas import tpu as pltpu
from jax.sharding import PartitionSpec as P

HEAD_DIM = 128
GROUPS = 4
MESH = pl.DeviceIdType.MESH
BF16 = jnp.bfloat16
F32 = jnp.float32


def remote(src, dst, send_sem, recv_sem, target):
    return pltpu.make_async_remote_copy(
        src_ref=src,
        dst_ref=dst,
        send_sem=send_sem,
        recv_sem=recv_sem,
        device_id=target,
        device_id_type=MESH,
    )


def await_bytes(ref, sem):
    pltpu.make_async_copy(ref, ref, sem).wait()


def flat_rows(block):
    cells, genes, cols = block.shape
    return block.astype(F32).reshape(cells * genes, cols).astype(BF16)


def far_first(i, n):
    return n // 2 + ((i + 1) // 2) * (1 - 2 * (i % 2))


def kernel(
    nz, nb, q, k, v, cot, w, counts, mixed_out, grad_out,
    stage, qkv, att_s, att_h, cot_v, cot_p, w_v, w_st, wz, wfull, counts_v, mixed_v, att_2d,
    mine, pair_s, pair_r, kept, two_s, two_r, rs_s, rs_r, z_32, z_s, z_r, row_s, row_r, grad_v,
    s_qkv, r_qkv, s_cot, r_cot, s_att, r_att, s_wf, r_wf, s_wn, r_wn, s_wa, r_wa, s_sib, r_sib,
    s_pair, r_pair, s_two, r_two, s_rs, r_rs, s_z, r_z, s_row, r_row, local_sem, out_sem,
):
    my_z, me = lax.axis_index("fsdp"), lax.axis_index("bal")
    core, chip = lax.rem(me, 2), me // 2
    sibling = {"bal": chip * 2 + (1 - core)}
    chips = nb // 2
    width = qkv.shape[-1]
    group_cols = width // GROUPS
    heads_per = group_cols // HEAD_DIM
    half_width = width // 2
    rows = nb * 8
    features = nz * nb
    high_n, low_n = wz.shape[0], wz.shape[1]
    high, low = my_z // low_n, lax.rem(my_z, low_n)
    x_n = 4
    x_at, y_at = lax.rem(chip, x_n), chip // x_n
    y_n = chips // x_n
    parity, z_half = lax.rem(my_z, 2), my_z // 2
    even_n = nz // 2
    next_z = {"fsdp": my_z + 1 - 2 * parity}

    def near(i):
        return high * low_n + lax.rem(low + i, low_n)

    def far(i):
        return lax.rem(high + i, high_n) * low_n + low

    def cols_of(g):
        return pl.ds(pl.multiple_of(g * group_cols, group_cols), group_cols)

    barrier = pltpu.get_barrier_semaphore()

    @pl.loop(1, nb)
    def _(i):
        pl.semaphore_signal(barrier, 1, device_id={"bal": lax.rem(me + i, nb)}, device_id_type=MESH)

    @pl.loop(1, even_n)
    def _(i):
        peer = lax.rem(z_half + i, even_n) * 2 + parity
        pl.semaphore_signal(barrier, 1, device_id={"fsdp": peer}, device_id_type=MESH)

    pl.semaphore_signal(barrier, 1, device_id=next_z, device_id_type=MESH)
    if low_n == 4:
        mirror = high * low_n + low_n - 1 - low
        pl.semaphore_signal(barrier, 1, device_id={"fsdp": mirror}, device_id_type=MESH)
    z_signals = even_n + (1 if low_n == 4 else 0)

    loads = [
        pltpu.make_async_copy(ref, stage.at[:, a], local_sem.at[a]) for a, ref in enumerate((q, k, v))
    ]
    load_w = pltpu.make_async_copy(w, w_v, local_sem.at[3])
    load_counts = pltpu.make_async_copy(counts, counts_v, local_sem.at[4])
    for load in (*loads, load_w, load_counts):
        load.start()

    load_w.wait()
    shard_tiles = w_st.shape[0]
    split = shard_tiles // 2 if y_n == x_n else shard_tiles
    x_cols = pl.ds(pl.multiple_of((x_at + x_n * core) * 128, 128), 128)
    y_cols = pl.ds(pl.multiple_of((y_at + x_n * core) * 128, 128), 128)
    kinds = [(0, split, x_cols)] + ([(split, shard_tiles, y_cols)] if split < shard_tiles else [])
    for first, last, at in kinds:
        part = w_v[first * 8 : last * 8, at].astype(F32)
        w_st[first:last] = part.reshape(last - first, 8, 128).astype(BF16)
    for load in loads:
        load.wait()
    pl.semaphore_wait(barrier, nb - 1 + z_signals)

    def send_qkv(g):
        cols = cols_of(g)
        pltpu.make_async_copy(stage.at[me, :, :, cols], qkv.at[me, :, :, cols], r_qkv.at[g]).start()

        @pl.loop(1, nb)
        def _(i):
            peer = lax.rem(me + i, nb)
            remote(
                stage.at[peer, :, :, cols], qkv.at[me, :, :, cols], s_qkv, r_qkv.at[g], {"bal": peer}
            ).start()

    send_qkv(0)
    pltpu.make_async_copy(w_st, wz.at[high, low], r_wf).start()
    for i in range(1, high_n):
        remote(w_st, wz.at[high, low], s_wf, r_wf, {"fsdp": far(i)}).start()
    pltpu.make_async_copy(cot.at[me], cot_v.at[me], r_cot).start()

    @pl.loop(1, nb)
    def _(i):
        peer = lax.rem(me + i, nb)
        remote(cot.at[peer], cot_v.at[me], s_cot, r_cot, {"bal": peer}).start()

    for g in range(1, GROUPS):
        send_qkv(g)

    load_counts.wait()

    my_counts = counts_v[pl.ds(me, 1), :].astype(F32)
    spread = lax.broadcasted_iota(jnp.int32, (rows, nb), 0) // 8 == lax.broadcasted_iota(
        jnp.int32, (rows, nb), 1
    )
    picked = jnp.where(spread, jnp.broadcast_to(my_counts, (rows, nb)), 0.0)
    row_count = jnp.sum(picked, axis=1, keepdims=True)
    slot = (lax.broadcasted_iota(jnp.int32, (rows, 1), 0) % 8).astype(F32)
    row_live = slot < row_count
    gather = (
        lax.broadcasted_iota(jnp.int32, (nb, rows), 1) // 8 == lax.broadcasted_iota(jnp.int32, (nb, rows), 0)
    )
    col_count = lax.dot_general(
        jnp.broadcast_to(my_counts, (8, nb)).astype(BF16),
        jnp.where(gather, 1.0, 0.0).astype(BF16),
        (((1,), (0,)), ((), ())),
        preferred_element_type=F32,
    )[0:1, :]
    col_slot = (lax.broadcasted_iota(jnp.int32, (1, rows), 1) % 8).astype(F32)
    col_live = col_slot < col_count
    scale = HEAD_DIM ** (-0.5)
    half_rows = features // 2
    plane_rows = half_rows // 2

    await_bytes(cot_v, r_cot)
    cot_2d = flat_rows(cot_v[...])
    step_rows = min(256, features)

    @pl.loop(0, features // step_rows)
    def _(n):
        shape = (step_rows, features)
        m = lax.broadcasted_iota(jnp.int32, shape, 0) + n * step_rows
        f = lax.broadcasted_iota(jnp.int32, shape, 1)
        z_of = (m % even_n) * 2 + (m // (even_n * chips)) % 2
        source = z_of * nb + ((m // even_n) % chips) * 2 + m // (nz * chips)
        chosen = jnp.where(f == source, 1.0, 0.0).astype(BF16)
        out = lax.dot_general(chosen, cot_2d, (((1,), (1,)), ((), ())), preferred_element_type=F32)
        cot_p[pl.ds(pl.multiple_of(n * step_rows, step_rows), step_rows), :] = out.astype(BF16)

    def attend(g):
        cols = cols_of(g)
        await_bytes(qkv.at[:, :, :, cols], r_qkv.at[g])

        for h in range(heads_per):
            head = pl.ds(pl.multiple_of(g * group_cols + h * HEAD_DIM, HEAD_DIM), HEAD_DIM)
            qh = flat_rows(qkv[:, 0, :, head])
            kh = flat_rows(qkv[:, 1, :, head])
            vh = flat_rows(qkv[:, 2, :, head])
            scores = lax.dot_general(qh, kh, (((1,), (1,)), ((), ())), preferred_element_type=F32)
            scores = jnp.where(col_live, scores * scale, -1e30)
            peak = jnp.max(scores, axis=1, keepdims=True)
            expo = jnp.exp(scores - peak)
            total = jnp.sum(expo, axis=1, keepdims=True)
            probs = (expo * (1.0 / total)).astype(BF16)
            out = lax.dot_general(probs, vh, (((1,), (0,)), ((), ())), preferred_element_type=F32)
            out = jnp.where(row_live, out, 0.0)
            out = out.astype(BF16)
            att_2d[:, head] = out
            att_s[:, :, head] = out.astype(F32).reshape(nb, 8, HEAD_DIM).astype(BF16)

    def share(g):
        cols = cols_of(g)
        a2 = att_2d[:, cols]
        their_rows = pl.ds(pl.multiple_of((1 - core) * half_rows, half_rows), half_rows)
        pair_s[g] = jnp.dot(cot_p[their_rows, :], a2, preferred_element_type=F32).astype(BF16)
        remote(pair_s.at[g], pair_r.at[g], s_pair, r_pair.at[g], sibling).start()
        my_rows = pl.ds(pl.multiple_of(core * half_rows, half_rows), half_rows)
        mine[g] = jnp.dot(cot_p[my_rows, :], a2, preferred_element_type=F32)

    def next_plane(g):
        await_bytes(pair_r.at[g], r_pair.at[g])
        theirs = pl.ds(pl.multiple_of((1 - parity) * plane_rows, plane_rows), plane_rows)
        two_s[g] = (mine[g, theirs, :] + pair_r[g, theirs, :].astype(F32)).astype(BF16)
        remote(two_s.at[g], two_r.at[g], s_two, r_two.at[g], next_z).start()
        ours = pl.ds(pl.multiple_of(parity * plane_rows, plane_rows), plane_rows)
        kept[g] = mine[g, ours, :] + pair_r[g, ours, :].astype(F32)

    def scatter(g):
        await_bytes(two_r.at[g], r_two.at[g])
        both = kept[g] + two_r[g].astype(F32)
        rs_s[g] = both.reshape(chips, even_n, group_cols).astype(BF16)
        pltpu.make_async_copy(rs_s.at[g, chip], rs_r.at[g, chip], r_rs.at[g]).start()

        @pl.loop(1, chips)
        def _(i):
            peer = lax.rem(chip + i, chips)
            remote(
                rs_s.at[g, peer], rs_r.at[g, chip], s_rs, r_rs.at[g], {"bal": peer * 2 + core}
            ).start()

    @pl.loop(0, GROUPS + 2)
    def _(t):
        @pl.when(t < GROUPS)
        def _():
            attend(t)
            share(t)

        @pl.when(jnp.logical_and(t >= 1, t < GROUPS + 1))
        def _():
            next_plane(t - 1)

        @pl.when(t >= 2)
        def _():
            scatter(t - 2)

        @pl.when(t == 0)
        def _():
            await_bytes(wz.at[:, low], r_wf)
            for i in range(1, low_n):
                remote(wz.at[:, low], wz.at[:, low], s_wn, r_wn, {"fsdp": near(i)}).start()

        @pl.when(t == 2)
        def _():
            await_bytes(wz.at[:, pl.ds(0, low_n - 1)], r_wn)
            for kind, (first, last, at) in enumerate(kinds):
                tiles = pl.ds(first, last - first)
                have = wz.at[:, :, tiles]
                place = wfull.at[:, :, tiles, :, at]
                pltpu.make_async_copy(have, place, r_wa).start()
                for i in range(1, x_n):
                    if kind == 0:
                        peer = (y_at * x_n + lax.rem(x_at + i, x_n)) * 2 + core
                    else:
                        peer = (lax.rem(y_at + i, y_n) * x_n + x_at) * 2 + core
                    remote(have, place, s_wa, r_wa, {"bal": peer}).start()

    for g in range(GROUPS):
        await_bytes(rs_r.at[g], r_rs.at[g])
        plane = jnp.sum(rs_r[g].astype(F32), axis=0)
        for t in range(group_cols // 128):
            z_32[pl.ds(g * (group_cols // 128) + t, even_n, stride=8), :] = plane[:, t * 128 : (t + 1) * 128]
    z_s[...] = z_32[...].reshape(z_s.shape).astype(BF16)
    pltpu.make_async_copy(z_s.at[z_half], z_r.at[z_half], r_z).start()

    @pl.loop(0, even_n - 1)
    def _(i):
        peer = lax.rem(z_half + far_first(i, even_n), even_n)
        remote(z_s.at[peer], z_r.at[z_half], s_z, r_z, {"fsdp": peer * 2 + parity}).start()

    pltpu.make_async_copy(att_s.at[me], att_h.at[me], r_att).start()

    @pl.loop(1, nb)
    def _(i):
        peer = lax.rem(me + i, nb)
        remote(att_s.at[peer], att_h.at[me], s_att, r_att, {"bal": peer}).start()

    my_half = wfull.at[:, :, :, :, pl.ds(pl.multiple_of(core * half_width, half_width), half_width)]
    await_bytes(my_half, r_wa)
    remote(my_half, my_half, s_sib, r_sib, sibling).start()

    await_bytes(z_r, r_z)
    row_s[...] = jnp.sum(z_r[...].astype(F32), axis=0)
    pltpu.make_async_copy(row_s, row_r.at[me], r_row).start()

    @pl.loop(1, nb)
    def _(i):
        peer = lax.rem(me + i, nb)
        remote(row_s, row_r.at[me], s_row, r_row, {"bal": peer}).start()

    await_bytes(my_half, r_sib)
    await_bytes(att_h, r_att)
    att_2d[...] = flat_rows(att_h[...])
    blocks = 2 if high_n % 2 == 0 else 1
    out_cols = blocks * low_n * nb

    @pl.loop(0, high_n // blocks)
    def _(n):
        wn = wfull[pl.ds(n * blocks, blocks)].astype(F32).reshape(out_cols, width).astype(BF16)
        out = lax.dot_general(att_2d[...], wn, (((1,), (1,)), ((), ())), preferred_element_type=F32)
        out_at = pl.ds(pl.multiple_of(n * out_cols, out_cols), out_cols)
        mixed_v[:, :, out_at] = out.reshape(nb, 8, out_cols).astype(BF16)

    store_mixed = pltpu.make_async_copy(mixed_v, mixed_out, out_sem.at[0])
    store_mixed.start()

    await_bytes(row_r, r_row)
    for t in range(8):
        grad_v[:, t * 128 : (t + 1) * 128] = row_r[:, t, :]
    store_grad = pltpu.make_async_copy(grad_v, grad_out, out_sem.at[1])
    store_grad.start()

    await_bytes(qkv.at[pl.ds(0, nb - 1)], s_qkv)
    await_bytes(att_s.at[pl.ds(0, nb - 1)], s_att)
    await_bytes(cot_v.at[pl.ds(0, nb - 1)], s_cot)
    await_bytes(wz.at[pl.ds(0, high_n - 1), 0], s_wf)
    await_bytes(wz.at[:, pl.ds(0, low_n - 1)], s_wn)
    await_bytes(wfull.at[:, :, :, :, pl.ds(0, (x_n - 1) * 128)], s_wa)
    await_bytes(my_half, s_sib)
    await_bytes(pair_s, s_pair)
    await_bytes(rs_s.at[:, pl.ds(0, chips - 1)], s_rs)
    await_bytes(two_s, s_two)
    await_bytes(z_s.at[pl.ds(0, even_n - 1)], s_z)
    await_bytes(row_r.at[pl.ds(0, nb - 1)], s_row)
    store_mixed.wait()
    store_grad.wait()


def local(nz, nb, query_rows, key_rows, value_rows, cotangent, out_weight, token_counts):
    cells, genes, width = query_rows.shape
    shard = out_weight.shape[0]
    features = nz * shard
    rows = cells * genes
    group_cols = width // GROUPS
    chips = nb // 2
    low_n = min(4, nz // 2)
    high_n = nz // low_n
    vmem = pltpu.VMEM
    dma = pltpu.SemaphoreType.DMA
    scratch = [
        vmem((nb, 3, genes, width), BF16),
        vmem((nb, 3, genes, width), BF16),
        vmem((nb, genes, width), BF16),
        vmem((nb, genes, width), BF16),
        vmem((nb, genes, features), BF16),
        vmem((features, rows), BF16),
        vmem((shard, width), BF16),
        vmem((shard // 8, 8, 128), BF16),
        vmem((high_n, low_n, shard // 8, 8, 128), BF16),
        vmem((high_n, low_n, shard // 8, 8, width), BF16),
        vmem(token_counts.shape, jnp.int32),
        vmem((nb, genes, features), BF16),
        vmem((rows, width), BF16),
        vmem((GROUPS, features // 2, group_cols), F32),
        vmem((GROUPS, features // 2, group_cols), BF16),
        vmem((GROUPS, features // 2, group_cols), BF16),
        vmem((GROUPS, features // 4, group_cols), F32),
        vmem((GROUPS, features // 4, group_cols), BF16),
        vmem((GROUPS, features // 4, group_cols), BF16),
        vmem((GROUPS, chips, nz // 2, group_cols), BF16),
        vmem((GROUPS, chips, nz // 2, group_cols), BF16),
        vmem((nz * 4, 128), F32),
        vmem((nz // 2, 8, 128), BF16),
        vmem((nz // 2, 8, 128), BF16),
        vmem((8, 128), F32),
        vmem((nb, 8, 128), F32),
        vmem((shard, width), F32),
        dma, dma((GROUPS,)),
        dma, dma,
        dma, dma,
        dma, dma,
        dma, dma,
        dma, dma,
        dma, dma,
        dma, dma((GROUPS,)),
        dma, dma((GROUPS,)),
        dma, dma((GROUPS,)),
        dma, dma,
        dma, dma,
        dma((5,)),
        dma((2,)),
    ]
    operands = (query_rows, key_rows, value_rows, cotangent, out_weight, token_counts)
    any_spec = pl.BlockSpec(memory_space=pl.ANY)
    return pl.pallas_call(
        functools.partial(kernel, nz, nb),
        out_shape=(
            jax.ShapeDtypeStruct((cells, genes, features), BF16),
            jax.ShapeDtypeStruct((shard, width), F32),
        ),
        in_specs=[any_spec] * 6,
        out_specs=(any_spec, any_spec),
        scratch_shapes=scratch,
        compiler_params=pltpu.CompilerParams(
            collective_id=0, has_side_effects=True, vmem_limit_bytes=48 * 1024 * 1024
        ),
        name="attend_project",
    )(*[pltpu.with_memory_space_constraint(a, pltpu.HBM) for a in operands])


def solution(mesh):
    nz, nb = mesh.shape["fsdp"], mesh.shape["bal"]
    placed = (
        P("fsdp", "bal", None),
        P("fsdp", "bal", None),
        P("fsdp", "bal", None),
        P("fsdp", "bal", None),
        P("fsdp", None),
        P("fsdp", None),
    )
    return jax.shard_map(
        functools.partial(local, nz, nb),
        mesh=mesh,
        in_specs=placed,
        out_specs=(P("fsdp", "bal", None), P("fsdp", None)),
        check_vma=False,
    )
```

```python
import functools

import jax
import jax.numpy as jnp
from jax import lax
from jax.experimental import pallas as pl
from jax.experimental.pallas import tpu as pltpu
from jax.sharding import PartitionSpec as P

HEAD_DIM = 128
GROUPS = 4
MESH = pl.DeviceIdType.MESH
BF16 = jnp.bfloat16
F32 = jnp.float32


def remote(src, dst, send_sem, recv_sem, target):
    return pltpu.make_async_remote_copy(
        src_ref=src,
        dst_ref=dst,
        send_sem=send_sem,
        recv_sem=recv_sem,
        device_id=target,
        device_id_type=MESH,
    )


def await_bytes(ref, sem):
    pltpu.make_async_copy(ref, ref, sem).wait()


def flat_rows(block):
    cells, genes, cols = block.shape
    return block.astype(F32).reshape(cells * genes, cols).astype(BF16)


def far_first(i, n):
    return n // 2 + ((i + 1) // 2) * (1 - 2 * (i % 2))


def kernel(
    nz, nb, q, k, v, cot, w, counts, mixed_out, grad_out,
    stage, qkv, att_s, att_h, cot_v, cot_p, w_v, w_st, wz, wfull, counts_v, mixed_v, att_2d,
    mine, pair_s, pair_r, kept, two_s, two_r, rs_s, rs_r, z_32, z_s, z_r, row_s, row_r, grad_v,
    s_qkv, r_qkv, s_cot, r_cot, s_att, r_att, s_wf, r_wf, s_wn, r_wn, s_wa, r_wa, s_sib, r_sib,
    s_pair, r_pair, s_two, r_two, s_rs, r_rs, s_z, r_z, s_row, r_row, local_sem, out_sem,
):
    my_z, me = lax.axis_index("fsdp"), lax.axis_index("bal")
    core, chip = lax.rem(me, 2), me // 2
    sibling = {"bal": chip * 2 + (1 - core)}
    chips = nb // 2
    width = qkv.shape[-1]
    group_cols = width // GROUPS
    heads_per = group_cols // HEAD_DIM
    half_width = width // 2
    rows = nb * 8
    features = nz * nb
    high_n, low_n = wz.shape[0], wz.shape[1]
    high, low = my_z // low_n, lax.rem(my_z, low_n)
    x_n = 4
    x_at, y_at = lax.rem(chip, x_n), chip // x_n
    y_n = chips // x_n
    parity, z_half = lax.rem(my_z, 2), my_z // 2
    even_n = nz // 2
    next_z = {"fsdp": my_z + 1 - 2 * parity}

    def near(i):
        return high * low_n + lax.rem(low + i, low_n)

    def far(i):
        return lax.rem(high + i, high_n) * low_n + low

    def cols_of(g):
        return pl.ds(pl.multiple_of(g * group_cols, group_cols), group_cols)

    barrier = pltpu.get_barrier_semaphore()

    @pl.loop(1, nb)
    def _(i):
        pl.semaphore_signal(barrier, 1, device_id={"bal": lax.rem(me + i, nb)}, device_id_type=MESH)

    @pl.loop(1, even_n)
    def _(i):
        peer = lax.rem(z_half + i, even_n) * 2 + parity
        pl.semaphore_signal(barrier, 1, device_id={"fsdp": peer}, device_id_type=MESH)

    pl.semaphore_signal(barrier, 1, device_id=next_z, device_id_type=MESH)
    if low_n == 4:
        mirror = high * low_n + low_n - 1 - low
        pl.semaphore_signal(barrier, 1, device_id={"fsdp": mirror}, device_id_type=MESH)
    z_signals = even_n + (1 if low_n == 4 else 0)

    loads = [
        pltpu.make_async_copy(ref, stage.at[:, a], local_sem.at[a]) for a, ref in enumerate((q, k, v))
    ]
    load_w = pltpu.make_async_copy(w, w_v, local_sem.at[3])
    load_counts = pltpu.make_async_copy(counts, counts_v, local_sem.at[4])
    for load in (*loads, load_w, load_counts):
        load.start()

    load_w.wait()
    shard_tiles = w_st.shape[0]
    split = shard_tiles // 2 if y_n == x_n else shard_tiles
    x_cols = pl.ds(pl.multiple_of((x_at + x_n * core) * 128, 128), 128)
    y_cols = pl.ds(pl.multiple_of((y_at + x_n * core) * 128, 128), 128)
    kinds = [(0, split, x_cols)] + ([(split, shard_tiles, y_cols)] if split < shard_tiles else [])
    for first, last, at in kinds:
        part = w_v[first * 8 : last * 8, at].astype(F32)
        w_st[first:last] = part.reshape(last - first, 8, 128).astype(BF16)
    for load in loads:
        load.wait()
    pl.semaphore_wait(barrier, nb - 1 + z_signals)

    def send_qkv(g):
        cols = cols_of(g)
        pltpu.make_async_copy(stage.at[me, :, :, cols], qkv.at[me, :, :, cols], r_qkv.at[g]).start()

        @pl.loop(1, nb)
        def _(i):
            peer = lax.rem(me + i, nb)
            remote(
                stage.at[peer, :, :, cols], qkv.at[me, :, :, cols], s_qkv, r_qkv.at[g], {"bal": peer}
            ).start()

    send_qkv(0)
    pltpu.make_async_copy(w_st, wz.at[high, low], r_wf).start()
    for i in range(1, high_n):
        remote(w_st, wz.at[high, low], s_wf, r_wf, {"fsdp": far(i)}).start()
    pltpu.make_async_copy(cot.at[me], cot_v.at[me], r_cot).start()

    @pl.loop(1, nb)
    def _(i):
        peer = lax.rem(me + i, nb)
        remote(cot.at[peer], cot_v.at[me], s_cot, r_cot, {"bal": peer}).start()

    for g in range(1, GROUPS):
        send_qkv(g)

    load_counts.wait()

    my_counts = counts_v[pl.ds(me, 1), :].astype(F32)
    spread = lax.broadcasted_iota(jnp.int32, (rows, nb), 0) // 8 == lax.broadcasted_iota(
        jnp.int32, (rows, nb), 1
    )
    picked = jnp.where(spread, jnp.broadcast_to(my_counts, (rows, nb)), 0.0)
    row_count = jnp.sum(picked, axis=1, keepdims=True)
    slot = (lax.broadcasted_iota(jnp.int32, (rows, 1), 0) % 8).astype(F32)
    row_live = slot < row_count
    gather = (
        lax.broadcasted_iota(jnp.int32, (nb, rows), 1) // 8 == lax.broadcasted_iota(jnp.int32, (nb, rows), 0)
    )
    col_count = lax.dot_general(
        jnp.broadcast_to(my_counts, (8, nb)).astype(BF16),
        jnp.where(gather, 1.0, 0.0).astype(BF16),
        (((1,), (0,)), ((), ())),
        preferred_element_type=F32,
    )[0:1, :]
    col_slot = (lax.broadcasted_iota(jnp.int32, (1, rows), 1) % 8).astype(F32)
    col_live = col_slot < col_count
    scale = HEAD_DIM ** (-0.5)
    half_rows = features // 2
    plane_rows = half_rows // 2

    await_bytes(cot_v, r_cot)
    cot_2d = flat_rows(cot_v[...])
    step_rows = min(256, features)

    @pl.loop(0, features // step_rows)
    def _(n):
        shape = (step_rows, features)
        m = lax.broadcasted_iota(jnp.int32, shape, 0) + n * step_rows
        f = lax.broadcasted_iota(jnp.int32, shape, 1)
        z_of = (m % even_n) * 2 + (m // (even_n * chips)) % 2
        source = z_of * nb + ((m // even_n) % chips) * 2 + m // (nz * chips)
        chosen = jnp.where(f == source, 1.0, 0.0).astype(BF16)
        out = lax.dot_general(chosen, cot_2d, (((1,), (1,)), ((), ())), preferred_element_type=F32)
        cot_p[pl.ds(pl.multiple_of(n * step_rows, step_rows), step_rows), :] = out.astype(BF16)

    def attend(g):
        cols = cols_of(g)
        await_bytes(qkv.at[:, :, :, cols], r_qkv.at[g])

        for h in range(heads_per):
            head = pl.ds(pl.multiple_of(g * group_cols + h * HEAD_DIM, HEAD_DIM), HEAD_DIM)
            qh = flat_rows(qkv[:, 0, :, head])
            kh = flat_rows(qkv[:, 1, :, head])
            vh = flat_rows(qkv[:, 2, :, head])
            scores = lax.dot_general(qh, kh, (((1,), (1,)), ((), ())), preferred_element_type=F32)
            scores = jnp.where(col_live, scores * scale, -1e30)
            peak = jnp.max(scores, axis=1, keepdims=True)
            expo = jnp.exp(scores - peak)
            total = jnp.sum(expo, axis=1, keepdims=True)
            probs = expo.astype(BF16)
            out = lax.dot_general(probs, vh, (((1,), (0,)), ((), ())), preferred_element_type=F32)
            out = jnp.where(row_live, out * (1.0 / total), 0.0)
            out = out.astype(BF16)
            att_2d[:, head] = out
            att_s[:, :, head] = out.astype(F32).reshape(nb, 8, HEAD_DIM).astype(BF16)

    def share(g):
        cols = cols_of(g)
        a2 = att_2d[:, cols]
        their_rows = pl.ds(pl.multiple_of((1 - core) * half_rows, half_rows), half_rows)
        pair_s[g] = jnp.dot(cot_p[their_rows, :], a2, preferred_element_type=F32).astype(BF16)
        remote(pair_s.at[g], pair_r.at[g], s_pair, r_pair.at[g], sibling).start()
        my_rows = pl.ds(pl.multiple_of(core * half_rows, half_rows), half_rows)
        mine[g] = jnp.dot(cot_p[my_rows, :], a2, preferred_element_type=F32)

    def next_plane(g):
        await_bytes(pair_r.at[g], r_pair.at[g])
        theirs = pl.ds(pl.multiple_of((1 - parity) * plane_rows, plane_rows), plane_rows)
        two_s[g] = (mine[g, theirs, :] + pair_r[g, theirs, :].astype(F32)).astype(BF16)
        remote(two_s.at[g], two_r.at[g], s_two, r_two.at[g], next_z).start()
        ours = pl.ds(pl.multiple_of(parity * plane_rows, plane_rows), plane_rows)
        kept[g] = mine[g, ours, :] + pair_r[g, ours, :].astype(F32)

    def scatter(g):
        await_bytes(two_r.at[g], r_two.at[g])
        both = kept[g] + two_r[g].astype(F32)
        rs_s[g] = both.reshape(chips, even_n, group_cols).astype(BF16)
        pltpu.make_async_copy(rs_s.at[g, chip], rs_r.at[g, chip], r_rs.at[g]).start()

        @pl.loop(1, chips)
        def _(i):
            peer = lax.rem(chip + i, chips)
            remote(
                rs_s.at[g, peer], rs_r.at[g, chip], s_rs, r_rs.at[g], {"bal": peer * 2 + core}
            ).start()

    @pl.loop(0, GROUPS + 2)
    def _(t):
        @pl.when(t < GROUPS)
        def _():
            attend(t)
            share(t)

        @pl.when(jnp.logical_and(t >= 1, t < GROUPS + 1))
        def _():
            next_plane(t - 1)

        @pl.when(t >= 2)
        def _():
            scatter(t - 2)

        @pl.when(t == 0)
        def _():
            await_bytes(wz.at[:, low], r_wf)
            for i in range(1, low_n):
                remote(wz.at[:, low], wz.at[:, low], s_wn, r_wn, {"fsdp": near(i)}).start()

        @pl.when(t == 2)
        def _():
            await_bytes(wz.at[:, pl.ds(0, low_n - 1)], r_wn)
            for kind, (first, last, at) in enumerate(kinds):
                tiles = pl.ds(first, last - first)
                have = wz.at[:, :, tiles]
                place = wfull.at[:, :, tiles, :, at]
                pltpu.make_async_copy(have, place, r_wa).start()
                for i in range(1, x_n):
                    if kind == 0:
                        peer = (y_at * x_n + lax.rem(x_at + i, x_n)) * 2 + core
                    else:
                        peer = (lax.rem(y_at + i, y_n) * x_n + x_at) * 2 + core
                    remote(have, place, s_wa, r_wa, {"bal": peer}).start()

    for g in range(GROUPS):
        await_bytes(rs_r.at[g], r_rs.at[g])
        plane = jnp.sum(rs_r[g].astype(F32), axis=0)
        for t in range(group_cols // 128):
            z_32[pl.ds(g * (group_cols // 128) + t, even_n, stride=8), :] = plane[:, t * 128 : (t + 1) * 128]
    z_s[...] = z_32[...].reshape(z_s.shape).astype(BF16)
    pltpu.make_async_copy(z_s.at[z_half], z_r.at[z_half], r_z).start()

    @pl.loop(0, even_n - 1)
    def _(i):
        peer = lax.rem(z_half + far_first(i, even_n), even_n)
        remote(z_s.at[peer], z_r.at[z_half], s_z, r_z, {"fsdp": peer * 2 + parity}).start()

    pltpu.make_async_copy(att_s.at[me], att_h.at[me], r_att).start()

    @pl.loop(1, nb)
    def _(i):
        peer = lax.rem(me + i, nb)
        remote(att_s.at[peer], att_h.at[me], s_att, r_att, {"bal": peer}).start()

    my_half = wfull.at[:, :, :, :, pl.ds(pl.multiple_of(core * half_width, half_width), half_width)]
    await_bytes(my_half, r_wa)
    remote(my_half, my_half, s_sib, r_sib, sibling).start()

    await_bytes(z_r, r_z)
    row_s[...] = jnp.sum(z_r[...].astype(F32), axis=0)
    pltpu.make_async_copy(row_s, row_r.at[me], r_row).start()

    @pl.loop(1, nb)
    def _(i):
        peer = lax.rem(me + i, nb)
        remote(row_s, row_r.at[me], s_row, r_row, {"bal": peer}).start()

    await_bytes(my_half, r_sib)
    await_bytes(att_h, r_att)
    att_2d[...] = flat_rows(att_h[...])
    blocks = 2 if high_n % 2 == 0 else 1
    out_cols = blocks * low_n * nb

    @pl.loop(0, high_n // blocks)
    def _(n):
        wn = wfull[pl.ds(n * blocks, blocks)].astype(F32).reshape(out_cols, width).astype(BF16)
        out = lax.dot_general(att_2d[...], wn, (((1,), (1,)), ((), ())), preferred_element_type=F32)
        out_at = pl.ds(pl.multiple_of(n * out_cols, out_cols), out_cols)
        mixed_v[:, :, out_at] = out.reshape(nb, 8, out_cols).astype(BF16)

    store_mixed = pltpu.make_async_copy(mixed_v, mixed_out, out_sem.at[0])
    store_mixed.start()

    await_bytes(row_r, r_row)
    for t in range(8):
        grad_v[:, t * 128 : (t + 1) * 128] = row_r[:, t, :]
    store_grad = pltpu.make_async_copy(grad_v, grad_out, out_sem.at[1])
    store_grad.start()

    await_bytes(qkv.at[pl.ds(0, nb - 1)], s_qkv)
    await_bytes(att_s.at[pl.ds(0, nb - 1)], s_att)
    await_bytes(cot_v.at[pl.ds(0, nb - 1)], s_cot)
    await_bytes(wz.at[pl.ds(0, high_n - 1), 0], s_wf)
    await_bytes(wz.at[:, pl.ds(0, low_n - 1)], s_wn)
    await_bytes(wfull.at[:, :, :, :, pl.ds(0, (x_n - 1) * 128)], s_wa)
    await_bytes(my_half, s_sib)
    await_bytes(pair_s, s_pair)
    await_bytes(rs_s.at[:, pl.ds(0, chips - 1)], s_rs)
    await_bytes(two_s, s_two)
    await_bytes(z_s.at[pl.ds(0, even_n - 1)], s_z)
    await_bytes(row_r.at[pl.ds(0, nb - 1)], s_row)
    store_mixed.wait()
    store_grad.wait()


def local(nz, nb, query_rows, key_rows, value_rows, cotangent, out_weight, token_counts):
    cells, genes, width = query_rows.shape
    shard = out_weight.shape[0]
    features = nz * shard
    rows = cells * genes
    group_cols = width // GROUPS
    chips = nb // 2
    low_n = min(4, nz // 2)
    high_n = nz // low_n
    vmem = pltpu.VMEM
    dma = pltpu.SemaphoreType.DMA
    scratch = [
        vmem((nb, 3, genes, width), BF16),
        vmem((nb, 3, genes, width), BF16),
        vmem((nb, genes, width), BF16),
        vmem((nb, genes, width), BF16),
        vmem((nb, genes, features), BF16),
        vmem((features, rows), BF16),
        vmem((shard, width), BF16),
        vmem((shard // 8, 8, 128), BF16),
        vmem((high_n, low_n, shard // 8, 8, 128), BF16),
        vmem((high_n, low_n, shard // 8, 8, width), BF16),
        vmem(token_counts.shape, jnp.int32),
        vmem((nb, genes, features), BF16),
        vmem((rows, width), BF16),
        vmem((GROUPS, features // 2, group_cols), F32),
        vmem((GROUPS, features // 2, group_cols), BF16),
        vmem((GROUPS, features // 2, group_cols), BF16),
        vmem((GROUPS, features // 4, group_cols), F32),
        vmem((GROUPS, features // 4, group_cols), BF16),
        vmem((GROUPS, features // 4, group_cols), BF16),
        vmem((GROUPS, chips, nz // 2, group_cols), BF16),
        vmem((GROUPS, chips, nz // 2, group_cols), BF16),
        vmem((nz * 4, 128), F32),
        vmem((nz // 2, 8, 128), BF16),
        vmem((nz // 2, 8, 128), BF16),
        vmem((8, 128), F32),
        vmem((nb, 8, 128), F32),
        vmem((shard, width), F32),
        dma, dma((GROUPS,)),
        dma, dma,
        dma, dma,
        dma, dma,
        dma, dma,
        dma, dma,
        dma, dma,
        dma, dma((GROUPS,)),
        dma, dma((GROUPS,)),
        dma, dma((GROUPS,)),
        dma, dma,
        dma, dma,
        dma((5,)),
        dma((2,)),
    ]
    operands = (query_rows, key_rows, value_rows, cotangent, out_weight, token_counts)
    any_spec = pl.BlockSpec(memory_space=pl.ANY)
    return pl.pallas_call(
        functools.partial(kernel, nz, nb),
        out_shape=(
            jax.ShapeDtypeStruct((cells, genes, features), BF16),
            jax.ShapeDtypeStruct((shard, width), F32),
        ),
        in_specs=[any_spec] * 6,
        out_specs=(any_spec, any_spec),
        scratch_shapes=scratch,
        compiler_params=pltpu.CompilerParams(
            collective_id=0, has_side_effects=True, vmem_limit_bytes=48 * 1024 * 1024
        ),
        name="attend_project",
    )(*[pltpu.with_memory_space_constraint(a, pltpu.HBM) for a in operands])


def solution(mesh):
    nz, nb = mesh.shape["fsdp"], mesh.shape["bal"]
    placed = (
        P("fsdp", "bal", None),
        P("fsdp", "bal", None),
        P("fsdp", "bal", None),
        P("fsdp", "bal", None),
        P("fsdp", None),
        P("fsdp", None),
    )
    return jax.shard_map(
        functools.partial(local, nz, nb),
        mesh=mesh,
        in_specs=placed,
        out_specs=(P("fsdp", "bal", None), P("fsdp", None)),
        check_vma=False,
    )
```
